32 devices in a mesh: tm: 8 (over z, x), space: 4 (over y, core).
Axes of the slice: x: 2, y: 2, z: 4, core: 2. Of those that a mesh axis runs over, the one named last changes fastest.
Arguments:
- states: float32 [8, 8, 24, 32, 128], P('tm', None, None, 'space'), may hold values from -6 to 6
- bio_matrix: float32 [8, 8], replicated, may hold values from -2 to 2
- uptake_rate: float32 [32, 128], P('space'), may hold values from 0.2 to 1
- mixing: float32 [23, 32, 128], P(None, 'space'), may hold values from 0.3 to 10
- land_sea: int32 [32, 128], P('space'), may hold values 0 or 1
- levels_active: int32 [32, 128], P('space'), may hold values from 1 to 24
Outputs:
- state_grad: float32 [8, 8, 24, 32, 128], P('tm', None, None, 'space')
- rate_grad: float32 [32, 128], P('space')
The draws below stay inside these ranges and needn't reach their ends.
All inputs are finite; a program needn't handle non-finite values. No bound on the sum of `land_sea` on one device may be relied on, other than what follows from the above.
Results may differ from the reference program's by a relative error of at most 0.0001.
Values sent between devices are 32-bit elements; how exact they have to be, the bound alone decides.
A program may use at most 64 MiB of HBM per device.

```python
import math
import jax
import jax.numpy as jnp
from jax import lax

TR = 8
K = 24
KM1 = 23
STEPS = 4
LON = 128
NLAT = 32
SLABS = 8
N_TM = 8


def set_ends(values, key, least, high):
    place = [jax.random.randint(jax.random.fold_in(key, axis), (), 0, length) for axis, length in enumerate(values.shape)]
    longest = values.shape.index(max(values.shape))
    beside = place[:longest] + [(place[longest] + 1) % values.shape[longest]] + place[longest + 1:]
    return values.at[tuple(place)].set(least).at[tuple(beside)].set(high)


def block_scale(key, dims, split, least, largest):
    loudness, own = 1.0, jax.random.fold_in(key, 6)
    for position, blocks in split:
        steps = jnp.exp(jax.random.uniform(jax.random.fold_in(own, position), (blocks,), jnp.float32, least / len(split), largest / len(split)))
        loudness = loudness * jnp.repeat(steps, dims[position] // blocks).reshape([-1 if axis == position else 1 for axis in range(len(dims))])
    return loudness


def gaussian(own_key, shape, spread, most, pieces=(), kind=jnp.bfloat16):
    factor_of = block_scale(own_key, shape, pieces, -0.22, 0.18) if pieces else 1.0
    values = jax.random.normal(own_key, shape, jnp.float32) * spread * factor_of
    return jnp.minimum(jnp.maximum(values, -most), most).astype(kind)


def setup_inputs(seed: int = 0) -> dict:
    splits = jax.random.split(jax.random.key(seed), 7)
    states = gaussian(splits[0], (SLABS, TR, K, NLAT, LON), 1.0, 6.0, ((0, 8), (3, 4)), jnp.float32)
    bio_matrix = gaussian(splits[1], (TR, TR), TR ** -0.5, 2.0, (), jnp.float32)
    uptake_rate = jnp.clip(jnp.exp(math.log(1.0) - 1.609438 * jax.random.uniform(splits[2], (NLAT, LON), jnp.float32) ** block_scale(splits[2], (NLAT, LON), ((0, 4),), -0.2, 0.2)), 0.2, 1.0)
    mixing = jnp.clip(jnp.exp(math.log(10.0) - 3.506558 * jax.random.uniform(splits[3], (KM1, NLAT, LON), jnp.float32) ** block_scale(splits[3], (KM1, NLAT, LON), ((1, 4),), -0.2, 0.2)), 0.3, 10.0)
    land_sea = set_ends((jax.random.randint(splits[4], (NLAT, LON), 0, 5) < 4).astype(jnp.int32), jax.random.fold_in(splits[4], 1), 0, 1)
    levels_active = set_ends(jax.random.randint(splits[5], (NLAT, LON), 1, K + 1), jax.random.fold_in(splits[5], 1), 1, K).astype(jnp.int32)
    return dict(states=states, bio_matrix=bio_matrix, uptake_rate=uptake_rate, mixing=mixing, land_sea=land_sea, levels_active=levels_active)


lateral_mix = 0.24
bio_step = 0.25

def vertical_factors(wet, mixing):
    couple = mixing * wet[:-1] * wet[1:]
    depth = wet.shape[0]
    pivots = []
    for height in range(depth):
        middle = 1.0 + jnp.zeros_like(wet[0])
        if height > 0:
            middle = middle + couple[height - 1]
        if height < depth - 1:
            middle = middle + couple[height]
        if height > 0:
            middle = middle - couple[height - 1] * couple[height - 1] / pivots[-1]
        pivots.append(middle)
    return (couple, pivots)

def column_solve(rhs, couple, pivots):
    depth = rhs.shape[1]
    sweep = [rhs[:, 0] / pivots[0]]
    for height in range(1, depth):
        sweep.append((rhs[:, height] + couple[height - 1] * sweep[-1]) / pivots[height])
    result = [sweep[depth - 1]]
    for height in range(depth - 2, -1, -1):
        result.append(sweep[height] + couple[height] / pivots[height] * result[-1])
    return jnp.stack(result[::-1], axis=1)

def shift_cols(field):
    zero_col = jnp.zeros(field.shape[:-1] + (1,), field.dtype)
    east_val = jnp.concatenate([field[..., 1:], zero_col], axis=-1)
    west_val = jnp.concatenate([zero_col, field[..., :-1]], axis=-1)
    return (east_val, west_val)

def face_factors(wet_pad):
    wet = wet_pad[:, 1:-1]
    east_val, west_val = shift_cols(wet)
    return (wet * wet_pad[:, 2:], wet * wet_pad[:, :-2], wet * east_val, wet * west_val)

def lateral_flux(field, padded, faces):
    east_val, west_val = shift_cols(field)
    total = faces[0] * (padded[:, :, 2:] - field) + faces[1] * (padded[:, :, :-2] - field)
    total = total + faces[2] * (east_val - field) + faces[3] * (west_val - field)
    return lateral_mix * total

def pad_rows(field):
    return jnp.pad(field, ((0, 0), (0, 0), (1, 1), (0, 0)))

def reference(states, bio_matrix, uptake_rate, mixing, land_sea, levels_active):
    heights = jnp.arange(K, dtype=jnp.int32)[:, None, None]
    wet = ((land_sea[None] == 1) & (heights < levels_active[None])).astype(jnp.float32)
    wet_pad = jnp.pad(wet, ((0, 0), (1, 1), (0, 0)))
    faces = face_factors(wet_pad)
    couple, pivots = vertical_factors(wet, mixing)

    def forward(start):
        field = start
        mixes = []
        for step_idx in range(STEPS):
            mixed = jnp.einsum('tu,ukln->tkln', bio_matrix, field, precision=lax.Precision.HIGHEST)
            mixes.append(mixed)
            star = wet * (field + lateral_flux(field, pad_rows(field), faces) + bio_step * uptake_rate * mixed)
            field = column_solve(star, couple, pivots)
        return (field, mixes)
    ends = lax.map(lambda start: forward(start)[0], states)
    defects = ends - wet * jnp.roll(states, -1, axis=0)

    def backward(pair):
        start, defect = pair
        unused, mixes = forward(start)
        lam = defect
        rate_term = jnp.zeros(uptake_rate.shape, jnp.float32)
        for step_idx in range(STEPS - 1, -1, -1):
            lstar = column_solve(lam, couple, pivots)
            rate_term = rate_term + bio_step * lax.optimization_barrier(jnp.sum(lstar * wet * mixes[step_idx], axis=(0, 1)))
            low = wet * lstar
            back_mix = jnp.einsum('tu,tkln->ukln', bio_matrix, low, precision=lax.Precision.HIGHEST)
            lam = low + lateral_flux(low, pad_rows(low), faces) + bio_step * uptake_rate * back_mix
        return (lam, rate_term)
    lams, rate_terms = lax.map(backward, (states, defects))
    state_grad = lams - jnp.roll(defects, 1, axis=0)
    scale = 1.0 / math.sqrt(STEPS * TR * K * N_TM)
    rate_grad = lax.optimization_barrier(jnp.sum(rate_terms, axis=0)) * scale
    return (state_grad, rate_grad)
```

```python
import functools
import math

import jax
import jax.numpy as jnp
from jax import lax
from jax.experimental import pallas as pl
from jax.experimental.pallas import tpu as pltpu
from jax.sharding import PartitionSpec as P

STEPS = 4
CHUNK = 8
BODY = 4

lateral_mix = 0.24
bio_step = 0.25


def kernel(n_tm, n_sp, states, bio, rate, mixing, land, levels, out, rate_out,
           x, sweep, defect, follow, earlier, halo, depths, depth_halo, coef, diag, wets, rates,
           halo_send, halo_recv, depth_send, depth_recv,
           follow_send, follow_recv, defect_send, defect_recv, rate_send, rate_recv):
    tracers, depth = states.shape[1], states.shape[2]
    lons = states.shape[4]
    chunks = depth // CHUNK
    tm, sp = lax.axis_index("tm"), lax.axis_index("space")
    nxt, prv = lax.rem(tm + 1, n_tm), lax.rem(tm + n_tm - 1, n_tm)
    has_up, has_down = sp > 0, sp < n_sp - 1
    near = ((has_up, sp - 1, 0, 1), (has_down, sp + 1, 7, 0))

    barrier = pltpu.get_barrier_semaphore()
    for has, other, _, _ in near:
        @pl.when(has)
        def _():
            pl.semaphore_signal(barrier, inc=1, device_id={"space": other},
                                device_id_type=pl.DeviceIdType.MESH)
    for d in range(1, n_tm):
        pl.semaphore_signal(barrier, inc=1, device_id={"tm": lax.rem(tm + d, n_tm)},
                            device_id_type=pl.DeviceIdType.MESH)

    tile = (8, lons)
    row = lax.broadcasted_iota(jnp.int32, tile, 0)
    lane = lax.broadcasted_iota(jnp.int32, tile, 1)
    top, bottom = row == 0, row == 7
    first, last = lane == 0, lane == lons - 1

    depths[...] = jnp.where(land[...] == 1, levels[...], 0).astype(jnp.float32)
    own_depth = depths[...]

    def wet_of(depth_map, k):
        return jnp.where(jnp.asarray(k, jnp.int32).astype(jnp.float32) < depth_map, 1.0, 0.0)

    def mask(k, _):
        w = wet_of(own_depth, k)
        wets[k] = w
        for t in range(tracers):
            x[0, t, k] = states[0, t, k] * w
        return 0

    lax.fori_loop(0, depth, mask, 0)
    for side, has in ((0, has_up), (1, has_down)):
        @pl.when(jnp.logical_not(has))
        def _():
            depth_halo[side] = jnp.zeros(tile, jnp.float32)

            def blank(i, _):
                for t in range(tracers):
                    halo[i, side, t] = jnp.zeros(halo.shape[3:], jnp.float32)
                return 0
            lax.fori_loop(0, halo.shape[0], blank, 0)

    pl.semaphore_wait(barrier, n_tm - 1 + has_up.astype(jnp.int32) + has_down.astype(jnp.int32))

    def depth_copy(other, side):
        return pltpu.make_async_remote_copy(
            depths, depth_halo.at[side], depth_send.at[side], depth_recv.at[side],
            device_id={"space": other}, device_id_type=pl.DeviceIdType.MESH)

    def halo_copy(j, c, other, edge, side):
        part = pl.ds(c * CHUNK, CHUNK)
        return pltpu.make_async_remote_copy(
            x.at[j, :, part, pl.ds(edge, 1), :], halo.at[j, side, :, part],
            halo_send.at[j, c, side], halo_recv.at[j, c, side],
            device_id={"space": other}, device_id_type=pl.DeviceIdType.MESH)

    def send_halo(j, c):
        for has, other, edge, side in near:
            @pl.when(has)
            def _():
                halo_copy(j, c, other, edge, side).start()

    def wait_halo(j, c):
        for has, other, edge, side in near:
            @pl.when(has)
            def _():
                halo_copy(j, c, other, edge, 1 - side).wait_recv()

    def follow_copy(c):
        part = pl.ds(c * CHUNK, CHUNK)
        return pltpu.make_async_remote_copy(
            states.at[0, :, part], follow.at[:, part], follow_send.at[c], follow_recv.at[c],
            device_id={"tm": prv}, device_id_type=pl.DeviceIdType.MESH)

    def defect_copy(c):
        part = pl.ds(c * CHUNK, CHUNK)
        return pltpu.make_async_remote_copy(
            defect.at[:, part], earlier.at[:, part], defect_send.at[c], defect_recv.at[c],
            device_id={"tm": nxt}, device_id_type=pl.DeviceIdType.MESH)

    def rate_copy(d):
        return pltpu.make_async_remote_copy(
            rates.at[tm], rates.at[tm], rate_send.at[d - 1], rate_recv.at[d - 1],
            device_id={"tm": lax.rem(tm + d, n_tm)}, device_id_type=pl.DeviceIdType.MESH)

    for has, other, edge, side in near:
        @pl.when(has)
        def _():
            depth_copy(other, side).start()
    for c in range(chunks):
        send_halo(0, c)
    for c in range(chunks):
        follow_copy(c).start()

    one = jnp.ones(tile, jnp.float32)

    def couple(k):
        if k < 0 or k >= depth - 1:
            return jnp.zeros(tile, jnp.float32)
        return mixing[k] * wets[k] * wets[k + 1]

    gain = [one, one]
    for i in range(depth):
        for way in range(2):
            k = i if way == 0 else depth - 1 - i
            behind, ahead = (couple(k - 1), couple(k)) if way == 0 else (couple(k), couple(k - 1))
            inv = 1.0 / (gain[way] + ahead)
            forth = ahead * inv
            coef[way, 0, k] = lateral_mix * wets[k] * inv
            coef[way, 1, k] = behind * inv
            coef[way, 2, k] = forth
            gain[way] = 1.0 + forth * gain[way]

    for has, other, edge, side in near:
        @pl.when(has)
        def _():
            depth_copy(other, 1 - side).wait_recv()
    zero = jnp.zeros(tile, jnp.float32)
    up_depth = jnp.where(top, depth_halo[0, 7:8, :], pltpu.roll(own_depth, 1, 0))
    down_depth = jnp.where(bottom, depth_halo[1, 0:1, :], pltpu.roll(own_depth, 7, 0))
    west_depth = jnp.where(first, zero, pltpu.roll(own_depth, 1, 1))
    east_depth = jnp.where(last, zero, pltpu.roll(own_depth, lons - 1, 1))

    def diagonal(k, _):
        count = (wet_of(up_depth, k) + wet_of(down_depth, k)
                 + wet_of(west_depth, k) + wet_of(east_depth, k))
        diag[k] = 1.0 / lateral_mix - count
        return 0

    lax.fori_loop(0, depth, diagonal, 0)
    bio_rate = rate[...] * (bio_step / lateral_mix)

    def mixed_of(field, back):
        result = []
        for t in range(tracers):
            total = None
            for u in range(tracers):
                term = field[u] * (bio[u, t] if back else bio[t, u])
                total = term if total is None else total + term
            result.append(total)
        return result

    def beside(v):
        return (jnp.where(first, zero, pltpu.roll(v, 1, 1))
                + jnp.where(last, zero, pltpu.roll(v, lons - 1, 1)))

    def across(v, j, t, k):
        return (jnp.where(top, halo[j, 0, t, k], pltpu.roll(v, 1, 0))
                + jnp.where(bottom, halo[j, 1, t, k], pltpu.roll(v, 7, 0)))

    def levels_loop(c, way, body, carry):
        def several(i, carry):
            for b in range(BODY):
                s = i * BODY + b
                k = c * CHUNK + (s if way == 0 else CHUNK - 1 - s)
                carry = body(k, carry)
            return carry
        return lax.fori_loop(0, CHUNK // BODY, several, carry)

    def order(way):
        return range(chunks) if way == 0 else range(chunks - 1, -1, -1)

    zeros = (zero,) * tracers

    def eliminate(j, way, back, rate_term):
        def body(k, carry):
            prev, rate_term = carry
            field = [x[j, t, k] for t in range(tracers)]
            mixed = mixed_of(field, back)
            if back:
                for t in range(tracers):
                    rate_term = rate_term + mixed[t] * x[7 - j, t, k]
            a, b, d = coef[way, 0, k], coef[way, 1, k], diag[k]
            now = []
            for t in range(tracers):
                v = field[t]
                star = v * d + bio_rate * mixed[t] + (beside(v) + across(v, j, t, k))
                s = star * a + b * prev[t]
                sweep[t, k] = s
                now.append(s)
            return tuple(now), rate_term

        carry = (zeros, rate_term)
        for c in order(way):
            wait_halo(j, c)
            carry = levels_loop(c, way, body, carry)
        return carry[1]

    def substitute(j, way):
        def body(k, prev):
            e = coef[way, 2, k]
            now = []
            for t in range(tracers):
                s = sweep[t, k] + e * prev[t]
                x[j, t, k] = s
                now.append(s)
            return tuple(now)

        carry = zeros
        for c in order(1 - way):
            carry = levels_loop(c, 1 - way, body, carry)
            send_halo(j, c)

    rate_term = zero
    for j in range(STEPS):
        way = j % 2
        eliminate(j, way, False, zero)
        if j < STEPS - 1:
            substitute(j + 1, way)

    def turn(k, carry):
        prev, held = carry
        e, w = coef[1, 2, k], wets[k]
        a, b = coef[0, 0, k] * (1.0 / lateral_mix), coef[0, 1, k]
        ends, now = [], []
        for t in range(tracers):
            v = sweep[t, k] + e * prev[t]
            gap = v - w * follow[t, k]
            defect[t, k] = gap
            s = gap * a + b * held[t]
            sweep[t, k] = s
            ends.append(v)
            now.append(s)
        return tuple(ends), tuple(now)

    carry = (zeros, zeros)
    for c in range(chunks):
        follow_copy(c).wait_recv()
        carry = levels_loop(c, 0, turn, carry)
        defect_copy(c).start()
    substitute(STEPS, 0)

    for j in range(STEPS, 2 * STEPS - 1):
        way = (j + 1) % 2
        rate_term = eliminate(j, way, True, rate_term)
        substitute(j + 1, way)

    end = 2 * STEPS - 1

    def finish_inner(k, rate_term):
        field = [x[end, t, k] for t in range(tracers)]
        mixed = mixed_of(field, True)
        for t in range(tracers):
            rate_term = rate_term + mixed[t] * x[0, t, k]
        for t in range(tracers):
            sweep[t, k] = field[t] * diag[k] + bio_rate * mixed[t] + beside(field[t])
        return rate_term

    for c in range(chunks):
        rate_term = levels_loop(c, 0, finish_inner, rate_term)
    rates[tm] = rate_term
    for d in range(1, n_tm):
        rate_copy(d).start()

    def finish(k, carry):
        w = wets[k] * lateral_mix
        for t in range(tracers):
            v = x[end, t, k]
            out[0, t, k] = w * (sweep[t, k] + across(v, end, t, k)) - earlier[t, k]
        return carry

    for c in range(chunks):
        wait_halo(end, c)
        defect_copy(c).wait_recv()
        levels_loop(c, 0, finish, 0)

    for d in range(1, n_tm):
        origin = lax.rem(tm + n_tm - d, n_tm)
        pltpu.make_async_remote_copy(
            rates.at[tm], rates.at[origin], rate_send.at[d - 1], rate_recv.at[d - 1],
            device_id={"tm": origin}, device_id_type=pl.DeviceIdType.MESH).wait_recv()
    total = rates[0]
    for d in range(1, n_tm):
        total = total + rates[d]
    rate_out[...] = total * (bio_step / math.sqrt(STEPS * tracers * depth * n_tm))

    for has, other, edge, side in near:
        @pl.when(has)
        def _():
            depth_copy(other, side).wait_send()
            for j in range(2 * STEPS):
                for c in range(chunks):
                    halo_copy(j, c, other, edge, side).wait_send()
    for c in range(chunks):
        follow_copy(c).wait_send()
        defect_copy(c).wait_send()
    for d in range(1, n_tm):
        rate_copy(d).wait_send()


def per_device(states, bio_matrix, uptake_rate, mixing, land_sea, levels_active):
    n_tm, n_sp = lax.axis_size("tm"), lax.axis_size("space")
    _, tracers, depth, rows, lons = states.shape
    chunks = depth // CHUNK
    vmem = pl.BlockSpec(memory_space=pltpu.VMEM)
    smem = pl.BlockSpec(memory_space=pltpu.SMEM)
    field = (tracers, depth, rows, lons)
    f32 = jnp.float32
    dma = pltpu.SemaphoreType.DMA
    return pl.pallas_call(
        functools.partial(kernel, n_tm, n_sp),
        out_shape=(jax.ShapeDtypeStruct(states.shape, f32), jax.ShapeDtypeStruct(uptake_rate.shape, f32)),
        in_specs=[vmem, smem, vmem, vmem, vmem, vmem],
        out_specs=(vmem, vmem),
        scratch_shapes=[
            pltpu.VMEM((2 * STEPS,) + field, f32),
            pltpu.VMEM(field, f32),
            pltpu.VMEM(field, f32),
            pltpu.VMEM(field, f32),
            pltpu.VMEM(field, f32),
            pltpu.VMEM((2 * STEPS, 2, tracers, depth, 1, lons), f32),
            pltpu.VMEM((rows, lons), f32),
            pltpu.VMEM((2, rows, lons), f32),
            pltpu.VMEM((2, 3, depth, rows, lons), f32),
            pltpu.VMEM((depth, rows, lons), f32),
            pltpu.VMEM((depth, rows, lons), f32),
            pltpu.VMEM((n_tm, rows, lons), f32),
            dma((2 * STEPS, chunks, 2)), dma((2 * STEPS, chunks, 2)),
            dma((2,)), dma((2,)),
            dma((chunks,)), dma((chunks,)),
            dma((chunks,)), dma((chunks,)),
            dma((n_tm - 1,)), dma((n_tm - 1,)),
        ],
        compiler_params=pltpu.CompilerParams(
            collective_id=0, has_side_effects=True, vmem_limit_bytes=40 * 1024 * 1024),
    )(states, bio_matrix, uptake_rate, mixing, land_sea, levels_active)


def solution(mesh):
    return jax.shard_map(
        per_device,
        mesh=mesh,
        in_specs=(
            P("tm", None, None, "space", None),
            P(),
            P("space", None),
            P(None, "space", None),
            P("space", None),
            P("space", None),
        ),
        out_specs=(P("tm", None, None, "space", None), P("space", None)),
        check_vma=False,
    )
```
